32 devices in a mesh: dp: 16 (over z, y, x), mp: 2 (over core).
Axes of the slice: x: 2, y: 2, z: 4, core: 2. Of those that a mesh axis runs over, the one named last changes fastest.
Arguments:
- field_ids: int32 [8192, 26], P('dp'), may hold values from 0 to 65535, as said below
- presence: int32 [8192, 39], P('dp'), may hold values 0 or 1
- dense: float32 [8192, 13], P('dp'), may hold values from -6 to 6
- labels: float32 [8192], P('dp'), may hold values from 0 to 1
- tables: bfloat16 [65536, 1014], P('dp', 'mp'), may hold values from -3 to 3
- cross_top: bfloat16 [2, 1014, 1027], P(None, 'mp'), may hold values from -0.1875 to 0.1875
- cross_tail: bfloat16 [2, 13, 1027], replicated, may hold values from -1.75 to 1.75
- cross_bias: float32 [2, 1027], replicated, may hold values from -2 to 2
- deep_top: bfloat16 [1014, 1024], P('mp'), may hold values from -0.1875 to 0.1875
- deep_tail: bfloat16 [13, 1024], replicated, may hold values from -1.75 to 1.75
- deep_second: bfloat16 [1024, 1024], P('mp'), may hold values from -0.1875 to 0.1875
- deep_bias: float32 [2, 1024], replicated, may hold values from -2 to 2
- out_embed: float32 [1014], P('mp'), may hold values from -0.375 to 0.375
- out_dense: float32 [13], replicated, may hold values from -3 to 3
- out_deep: float32 [1024], replicated, may hold values from -0.375 to 0.375
- out_bias: float32 [1], replicated, may hold values from -2 to 2
Outputs:
- grad_embedded: float32 [8192, 1014], P('dp', 'mp')
- grad_dense: float32 [8192, 13], P('dp')
- grad_tables: float32 [65536, 1014], P('dp', 'mp')
- grad_cross_top: float32 [2, 1014, 1027], P(None, 'mp')
- grad_cross_tail: float32 [2, 13, 1027], replicated
- grad_cross_bias: float32 [2, 1027], replicated
- grad_deep_top: float32 [1014, 1024], P('mp')
- grad_deep_tail: float32 [13, 1024], replicated
- grad_deep_second: float32 [1024, 1024], P('mp')
- grad_deep_bias: float32 [2, 1024], replicated
- grad_out_embed: float32 [1014], P('mp')
- grad_out_dense: float32 [13], replicated
- grad_out_deep: float32 [1024], replicated
- grad_out_bias: float32 [1], replicated
The draws below stay inside these ranges and needn't reach their ends.
Inputs may be any that keep to these rules, and one draw needn't show every extreme that they name: `field_ids`: among the examples of one index of dp, each block of table rows k * 4096 to (k + 1) * 4096 - 1 is named by exactly 32 examples in each field.
All inputs are finite; a program needn't handle non-finite values. No bound on the sum of `presence` on one device may be relied on, other than what follows from the above.
Results may differ from the reference program's by a relative error of at most 0.012.
The reference program's roundings to bfloat16 on the way count: a program that leaves them out, or rounds other values in their place, can miss the bound.
Values may be sent and summed in bfloat16 or wider, within the bound.
A program may use at most 448 MiB of HBM per device.

```python
import math
import jax
import jax.numpy as jnp
from jax import lax

FIELDS = 26
EMBED = 39
DENSE = 13
HIDDEN_SIZE = 1024
VOCAB = 65536
LAYERS = 2
EX_DEV = 512
EMB_W = 1014
D = 1027
EXAMPLES = 8192
ROWS_OWN = 4096


def draw_field_ids(key, part):
    key = jax.random.fold_in(key, 11)
    key_owner, key_row = jax.random.split(key, 2)
    blocks = EXAMPLES // EX_DEV
    owner_keys = jax.random.split(key_owner, blocks * FIELDS)
    orders = jax.vmap(lambda single: jax.random.permutation(single, EX_DEV))(owner_keys)
    owners = (orders % blocks).reshape(blocks, FIELDS, EX_DEV)
    owners = jnp.transpose(owners, (0, 2, 1)).reshape(EXAMPLES, FIELDS)
    local_rows = jax.random.randint(key_row, (EXAMPLES, FIELDS), 0, ROWS_OWN)
    return (owners * ROWS_OWN + local_rows).astype(jnp.int32)


def with_ends(drawn, stream_key, least, largest):
    spot = [jax.random.randint(jax.random.fold_in(stream_key, axis), (), 0, length) for axis, length in enumerate(drawn.shape)]
    main_axis = drawn.shape.index(max(drawn.shape))
    next_to = spot[:main_axis] + [(spot[main_axis] + 1) % drawn.shape[main_axis]] + spot[main_axis + 1:]
    return drawn.at[tuple(spot)].set(least).at[tuple(next_to)].set(largest)


def steps_of(stream_key, dims, pieces, low, largest):
    loudness, own = 1.0, jax.random.fold_in(stream_key, 6)
    for axis_at, parts in pieces:
        heights = jnp.exp(jax.random.uniform(jax.random.fold_in(own, axis_at), (parts,), jnp.float32, low / len(pieces), largest / len(pieces)))
        loudness = loudness * jnp.repeat(heights, dims[axis_at] // parts).reshape([-1 if axis == axis_at else 1 for axis in range(len(dims))])
    return loudness


def scatter_about(rng, extent, scale, bound, cuts=(), kind=jnp.bfloat16):
    result = jax.random.normal(rng, extent, jnp.float32) * scale
    if len(cuts) > 0:
        result = steps_of(rng, extent, cuts, -0.22, 0.18) * result
    return jnp.clip(result, min=-bound, max=bound).astype(kind)


def setup_inputs(seed: int = 0) -> dict:
    arg_keys = jax.random.split(jax.random.key(seed), 17)
    field_ids = draw_field_ids(jax.random.fold_in(arg_keys[16], 71), 0)
    presence = with_ends((jax.random.randint(arg_keys[1], (EXAMPLES, FIELDS + DENSE), 0, 10) < 9).astype(jnp.int32), jax.random.fold_in(arg_keys[1], 1), 0, 1)
    dense = scatter_about(arg_keys[2], (EXAMPLES, DENSE), 1.0, 6.0, ((0, 16),), jnp.float32)
    labels = jnp.clip(1.0 * jax.random.uniform(arg_keys[3], (EXAMPLES,), jnp.float32) ** steps_of(arg_keys[3], (EXAMPLES,), ((0, 16),), -0.2, 0.2), 0.0, 1.0)
    tables = scatter_about(arg_keys[4], (VOCAB, EMB_W), 0.5, 3.0, ((0, 16), (1, 2)))
    cross_top = scatter_about(arg_keys[5], (LAYERS, EMB_W, D), D ** -0.5, 0.1875, ((1, 2),))
    cross_tail = scatter_about(arg_keys[6], (LAYERS, DENSE, D), DENSE ** -0.5, 1.75)
    cross_bias = scatter_about(arg_keys[7], (LAYERS, D), 0.3, 2.0, (), jnp.float32)
    deep_top = scatter_about(arg_keys[8], (EMB_W, HIDDEN_SIZE), D ** -0.5, 0.1875, ((0, 2),))
    deep_tail = scatter_about(arg_keys[9], (DENSE, HIDDEN_SIZE), DENSE ** -0.5, 1.75)
    deep_second = scatter_about(arg_keys[10], (HIDDEN_SIZE, HIDDEN_SIZE), HIDDEN_SIZE ** -0.5, 0.1875, ((0, 2),))
    deep_bias = scatter_about(arg_keys[11], (2, HIDDEN_SIZE), 0.3, 2.0, (), jnp.float32)
    out_embed = scatter_about(arg_keys[12], (EMB_W,), 256 ** -0.5, 0.375, ((0, 2),), jnp.float32)
    out_dense = scatter_about(arg_keys[13], (DENSE,), 4 ** -0.5, 3.0, (), jnp.float32)
    out_deep = scatter_about(arg_keys[14], (HIDDEN_SIZE,), 256 ** -0.5, 0.375, (), jnp.float32)
    out_bias = scatter_about(arg_keys[15], (1,), 0.5, 2.0, (), jnp.float32)
    return {"field_ids": field_ids, "presence": presence, "dense": dense, "labels": labels, "tables": tables, "cross_top": cross_top, "cross_tail": cross_tail, "cross_bias": cross_bias, "deep_top": deep_top, "deep_tail": deep_tail, "deep_second": deep_second, "deep_bias": deep_bias, "out_embed": out_embed, "out_dense": out_dense, "out_deep": out_deep, "out_bias": out_bias}


@jax.custom_vjp
def low(v):
    return lax.optimization_barrier(v.astype(jnp.bfloat16)).astype(jnp.float32)

@jax.custom_vjp
def low_back(v):
    return v

def low_keep(v):
    return (low(v), None)

def low_pass(kept, grad):
    return (grad,)

def back_keep(v):
    return (v, None)

def back_low(kept, grad):
    return (low(grad),)
low.defvjp(low_keep, low_pass)
low_back.defvjp(back_keep, back_low)

def product(left, right):
    return jnp.dot(left, right, precision=lax.Precision.HIGHEST)

def block_loss(embed_rows, tail_rows, label_rows, weights):
    cross_up, cross_low, cross_shift, deep_up, deep_low, deep_mid, deep_shift, head_embed, head_dense, head_deep, head_shift = weights
    x0_embed = low_back(embed_rows)
    x0_tail = low(tail_rows)
    anchor = jnp.concatenate([x0_embed, x0_tail], axis=1)
    state = anchor
    for layer in range(2):
        matrix = jnp.concatenate([cross_up[layer], cross_low[layer]], axis=0)
        mixing = low_back(product(low(state), matrix) + cross_shift[layer])
        state = anchor * mixing + state
    first_pre = low_back(product(anchor, jnp.concatenate([deep_up, deep_low], axis=0)) + deep_shift[0])
    first_act = low(low_back(jax.nn.gelu(first_pre)))
    second_pre = low_back(product(first_act, deep_mid) + deep_shift[1])
    second_act = jax.nn.gelu(second_pre)
    logits = product(state, jnp.concatenate([head_embed, head_dense])) + product(second_act, head_deep) + head_shift[0]
    return jnp.sum(jax.nn.softplus(logits) - label_rows * logits)

def reference(field_ids, presence, dense, labels, tables, cross_top, cross_tail, cross_bias, deep_top, deep_tail, deep_second, deep_bias, out_embed, out_dense, out_deep, out_bias):
    present = presence[:, :FIELDS] == 1
    used_ids = jnp.where(present, field_ids, 0).astype(jnp.int32)
    columns = jnp.arange(FIELDS, dtype=jnp.int32)[None, :]

    def lookup(table_values):
        shaped = table_values.reshape(VOCAB, FIELDS, EMBED)
        return shaped[used_ids, columns].reshape(EXAMPLES, FIELDS * EMBED)
    embedded, table_back = jax.vjp(lookup, tables.astype(jnp.float32))
    tail_input = dense * presence[:, FIELDS:].astype(jnp.float32)
    weights = (cross_top.astype(jnp.float32), cross_tail.astype(jnp.float32), cross_bias, deep_top.astype(jnp.float32), deep_tail.astype(jnp.float32), deep_second.astype(jnp.float32), deep_bias, out_embed, out_dense, out_deep, out_bias)
    block_rows = math.gcd(EXAMPLES, 4096)
    blocks = EXAMPLES // block_rows
    inputs = (embedded.reshape(blocks, block_rows, FIELDS * EMBED), tail_input.reshape(blocks, block_rows, DENSE), labels.reshape(blocks, block_rows))

    def one_block(totals, block):
        embed_rows, tail_rows, label_rows = block

        def partial_loss(embed_arg, tail_arg, weight_arg):
            return block_loss(embed_arg, tail_arg, label_rows, weight_arg)
        value, pull_back = jax.vjp(partial_loss, embed_rows, tail_rows, weights)
        grad_embed, grad_tail, grad_weights = pull_back(jnp.ones_like(value))
        totals = jax.tree.map(lambda earlier, latest: earlier + latest, totals, grad_weights)
        return (totals, (grad_embed, grad_tail))
    zeros_start = jax.tree.map(jnp.zeros_like, weights)
    totals, (grad_embed, grad_tail) = lax.scan(one_block, zeros_start, inputs)
    grad_embedded = grad_embed.reshape(EXAMPLES, FIELDS * EMBED)
    grad_dense = grad_tail.reshape(EXAMPLES, DENSE)
    grad_tables = table_back(grad_embedded)[0]
    g_top, g_tail, g_cbias, g_dtop, g_dtail, g_second, g_dbias, g_oembed, g_odense, g_odeep, g_obias = totals
    return (grad_embedded, grad_dense, grad_tables, g_top, g_tail, g_cbias, g_dtop, g_dtail, g_second, g_dbias, g_oembed, g_odense, g_odeep, g_obias)
```

```python
import math

import jax
import jax.numpy as jnp
from jax import lax
from jax.experimental import pallas as pl
from jax.experimental.pallas import tpu as pltpu
from jax.sharding import PartitionSpec as P

MESH = pl.DeviceIdType.MESH
GELU_SCALE = math.sqrt(2.0 / math.pi)
GELU_CUBE = 0.044715
CHUNK = 32
LANES = 128
UNIT = 512
REST_UNIT = 256
LOW_ROWS = 256
REST_ROWS = 48
WIDE, LOW = jnp.float32, jnp.bfloat16


def product(left, right):
    return jnp.dot(left, right, preferred_element_type=jnp.float32)


def product_t(left, right):
    return lax.dot_general(
        left, right, (((1,), (1,)), ((), ())), preferred_element_type=jnp.float32
    )


def product_tn(left, right):
    return lax.dot_general(
        left, right, (((0,), (0,)), ((), ())), preferred_element_type=jnp.float32
    )


def gelu_parts(value):
    square = value * value
    bend = jnp.tanh(GELU_SCALE * (value + GELU_CUBE * (square * value)))
    slope = GELU_SCALE * (1.0 + (3.0 * GELU_CUBE) * square)
    act = value * (0.5 * (1.0 + bend))
    grad = 0.5 * (1.0 + bend) + 0.5 * value * (1.0 - bend * bend) * slope
    return act, grad


def tile_of(field, width):
    return (field * width) // LANES * LANES


def inside(field, width, at):
    lane = lax.broadcasted_iota(jnp.int32, (1, LANES), 1) + at * LANES
    return (lane >= field * width) & (lane < (field + 1) * width)


def ready_after(field, fields, width, chunks):
    return chunks if field == fields - 1 else tile_of(field + 1, width) // LANES


def spread_of(marks, width, total):
    fields = marks.shape[1]
    row = lax.broadcasted_iota(jnp.int32, (fields, total), 0)
    lane = lax.broadcasted_iota(jnp.int32, (fields, total), 1)
    spread = ((lane >= row * width) & (lane < (row + 1) * width)).astype(LOW)
    return product(marks, spread)


def counting(shape, axis):
    return lax.broadcasted_iota(jnp.int32, shape, axis).astype(WIDE).astype(LOW)


def equal(left, right):
    return jnp.where(left == right, jnp.ones((), LOW), jnp.zeros((), LOW))


def key_of(index, part):
    return jnp.where((index >> 8) == part, index & 255, -1).astype(WIDE)


def layers_apart(pairs):
    rows = pairs.shape[0]
    at = lax.broadcasted_iota(jnp.int32, (2 * rows, 2 * rows), 0)
    source = lax.broadcasted_iota(jnp.int32, (2 * rows, 2 * rows), 1)
    wanted = jnp.where(at < rows, 2 * at, 2 * (at - rows) + 1)
    order = (source == wanted).astype(LOW)
    return product(order, pairs.reshape(2 * rows, pairs.shape[2])).astype(LOW)


def by_field(fields, width, chunks, take):
    pieces = [None] * chunks
    for field in range(fields):
        start = tile_of(field, width)
        wide = min(2 * LANES, chunks * LANES - start)
        found = take(field, start, wide)
        for piece in range(wide // LANES):
            at = start // LANES + piece
            part = found[:, piece * LANES : (piece + 1) * LANES]
            pieces[at] = (
                part
                if pieces[at] is None
                else jnp.where(inside(field, width, at), part, pieces[at])
            )
    return jnp.concatenate(pieces, axis=1)


def scattered(asked, back, first_part, parts, fields, width):
    chunks = back.shape[0]
    points = asked.shape[1]
    low_row = counting((LOW_ROWS, 1), 0)

    def picked(field, start, wide):
        index = asked[field : field + 1, :]
        pick = jnp.concatenate(
            [equal(key_of(index, first_part + part).astype(LOW), low_row) for part in range(parts)],
            axis=0,
        )
        window = [
            back[start // LANES + piece].reshape(points, LANES) for piece in range(wide // LANES)
        ]
        return product(pick, jnp.concatenate(window, axis=1))

    return by_field(fields, width, chunks, picked)


def shares_of(table_rows):
    block_rows = min(table_rows, 4 * LOW_ROWS)
    blocks = table_rows // block_rows
    return block_rows, blocks - blocks // 4, blocks // 4


def plan_of(rows, order):
    steps, size = [], rows
    for bit in order:
        if isinstance(bit, tuple):
            size //= 4
            steps.append(("spread", bit[0], size))
        elif size // 2 >= 16 and (size // 2) % 16 == 0:
            size //= 2
            steps.append(("halve", bit, size))
        else:
            steps.append(("both", bit, size))
    for kind, bit, size in reversed(list(steps)):
        if kind != "both":
            steps.append(("join" if kind == "halve" else "gather", bit, size))
    return steps


def copies_in(step):
    return 3 if step[0] in ("spread", "gather") else 1


def held_rows(rows, order):
    return sum(
        copies_in(step) * step[2] for step in plan_of(rows, order) if step[0] not in ("join", "gather")
    )


def train_kernel(
    streams,
    moments,
    ids_ref,
    presence_ref,
    dense_ref,
    label_ref,
    tables_ref,
    cross_ref,
    deep_ref,
    second_ref,
    cross_tail_ref,
    cross_bias_ref,
    deep_tail_ref,
    deep_bias_ref,
    out_embed_ref,
    out_dense_ref,
    out_deep_ref,
    out_bias_ref,
    units_out_ref,
    rest_out_ref,
    small_out_ref,
    embed_out_ref,
    dense_out_ref,
    table_out_ref,
    asked_out_ref,
    back_out_ref,
    table_ref,
    found_ref,
    came_ref,
    first_rows_ref,
    ids_came_ref,
    asked_rows_ref,
    id_cols_ref,
    raw_ref,
    w_cross_ref,
    w_deep_ref,
    w_second_ref,
    w_tail_ref,
    head_ref,
    emb_all_ref,
    tail_all_ref,
    x_parts_ref,
    x1_parts_ref,
    x1_tail_ref,
    h_low_ref,
    anchor_ref,
    state_ref,
    mix_one_ref,
    mix_two_ref,
    pre_one_ref,
    pre_two_ref,
    slope_one_ref,
    back_one_ref,
    back_hidden_ref,
    g_col_ref,
    label_col_ref,
    x1_all_ref,
    x1t_all_ref,
    x1_send_ref,
    h_all_ref,
    h_send_ref,
    dz_one_ref,
    dz_two_ref,
    da_one_ref,
    da_two_ref,
    ge_all_ref,
    gd_all_ref,
    part_send_ref,
    part_recv_ref,
    rest_ref,
    back_ref,
    place_keys_ref,
    units_ref,
    rest_low_ref,
    units_all_ref,
    rest_all_ref,
    units_got_ref,
    rest_got_ref,
    small_acc_ref,
    small_got_ref,
    load_sem_ref,
    ids_send_ref,
    ids_recv_ref,
    rows_send_ref,
    rows_recv_ref,
    row_send_ref,
    row_recv_ref,
    pair_send_ref,
    pair_recv_ref,
    sum_send_ref,
    sum_recv_ref,
    small_send_ref,
    small_recv_ref,
    store_sem_ref,
    back_send_ref,
    back_recv_ref,
    table_sem_ref,
    back_store_ref,
):
    place, mine = lax.axis_index("dp"), lax.axis_index("mp")
    peer = 1 - mine
    first = mine == 0
    fields_all, examples = ids_ref.shape
    fields = fields_all // 2
    table_rows, local = tables_ref.shape
    width = local // fields
    embed = 2 * local
    half = examples // 2
    hidden = second_ref.shape[0]
    main = deep_ref.shape[1]
    dense = dense_ref.shape[0]
    full = cross_bias_ref.shape[1]
    count, padded, slots = ids_came_ref.shape
    points = count * slots
    chunks = found_ref.shape[0]
    span = chunks * LANES
    bits = count.bit_length() - 1
    my_rows = pl.ds(pl.multiple_of(mine * half, half), half)
    peer_rows = pl.ds(pl.multiple_of(peer * half, half), half)

    def other(step):
        return lax.rem(place + step, count)

    def every(action):
        def one(step, unused):
            action(step)
            return unused

        lax.fori_loop(1, count, one, 0)

    pair = {}

    def send(number, source, target):
        pair[number] = pltpu.make_async_remote_copy(
            src_ref=source,
            dst_ref=target,
            send_sem=pair_send_ref.at[number],
            recv_sem=pair_recv_ref.at[number],
            device_id={"mp": peer},
            device_id_type=MESH,
        )
        pair[number].start()

    loads = []

    def load(source, target):
        loads.append(pltpu.make_async_copy(source, target, load_sem_ref.at[len(loads)]))
        loads[-1].start()
        return loads[-1]

    barrier = pltpu.get_barrier_semaphore()
    every(
        lambda step: pl.semaphore_signal(
            barrier, inc=1, device_id={"dp": other(step)}, device_id_type=MESH
        )
    )
    pl.semaphore_signal(barrier, inc=1, device_id={"mp": peer}, device_id_type=MESH)
    table_load = load(tables_ref, table_ref)
    raw_load = load(cross_ref, raw_ref)
    deep_load = load(deep_ref, w_deep_ref.at[mine])
    second_load = load(second_ref, w_second_ref.at[mine])

    ids = jnp.where(first, ids_ref[:fields, :], ids_ref[fields:, :])
    here = jnp.where(first, presence_ref[:fields, :], presence_ref[fields:fields_all, :])
    owner = ids // table_rows
    row_in = ids - owner * table_rows
    total = fields * count
    row_field = lax.broadcasted_iota(jnp.int32, (total, fields), 0) // count
    lane_field = lax.broadcasted_iota(jnp.int32, (total, fields), 1)
    widen = (row_field == lane_field).astype(LOW)
    owners = product(widen, owner.astype(WIDE).astype(LOW))
    row_owner = lax.broadcasted_iota(jnp.int32, (total, 1), 0)
    row_owner = (row_owner - row_owner // count * count).astype(WIDE)
    chosen = (owners == row_owner).astype(WIDE)
    early = lax.broadcasted_iota(jnp.int32, (examples, examples), 0)
    late = lax.broadcasted_iota(jnp.int32, (examples, examples), 1)
    before = product(chosen.astype(LOW), (early < late).astype(LOW))
    rank = product_tn(widen, (before * chosen).astype(LOW))
    place_rows = owner * slots + rank.astype(jnp.int32)
    spare = jnp.zeros((padded - fields, examples), jnp.int32)
    place_cols = jnp.concatenate([place_rows, spare], axis=0).T
    row_cols = jnp.concatenate([row_in, spare], axis=0).T
    point = lax.broadcasted_iota(jnp.int32, (1, points), 1)
    for field in range(fields):
        taken = jnp.where(
            place_cols[:, field : field + 1] == point, row_cols[:, field : field + 1], 0
        )
        asked_rows_ref[field : field + 1, :] = jnp.sum(taken, axis=0, keepdims=True)
    asked_rows_ref[fields:, :] = jnp.zeros((padded - fields, points), jnp.int32)
    for target in range(count):
        id_cols_ref[target] = asked_rows_ref[:, target * slots : (target + 1) * slots]
    pl.semaphore_wait(barrier, count)

    def ids_copy(step):
        return pltpu.make_async_remote_copy(
            src_ref=id_cols_ref.at[other(step)],
            dst_ref=ids_came_ref.at[place],
            send_sem=ids_send_ref.at[step],
            recv_sem=ids_recv_ref.at[step],
            device_id={"dp": other(step)},
            device_id_type=MESH,
        )

    def row_copy(step):
        return pltpu.make_async_remote_copy(
            src_ref=table_ref.at[pl.ds(0, 16)],
            dst_ref=first_rows_ref,
            send_sem=row_send_ref.at[step],
            recv_sem=row_recv_ref,
            device_id={"dp": other(step)},
            device_id_type=MESH,
        )

    def rows_copy(chunk, step):
        return pltpu.make_async_remote_copy(
            src_ref=found_ref.at[chunk, other(step)],
            dst_ref=came_ref.at[chunk, place],
            send_sem=rows_send_ref.at[chunk, step],
            recv_sem=rows_recv_ref.at[chunk, step],
            device_id={"dp": other(step)},
            device_id_type=MESH,
        )

    every(lambda step: ids_copy(step).start())
    ids_came_ref[place] = id_cols_ref[place]
    send(0, deep_ref, w_deep_ref.at[mine])
    send(1, second_ref, w_second_ref.at[mine])
    table_load.wait()

    @pl.when(place == 0)
    def _():
        every(lambda step: row_copy(step).start())

    packed = units_all_ref
    wide = table_rows // LOW_ROWS * width
    def pack(field):
        for high in range(table_rows // LOW_ROWS):
            packed[
                field // 2,
                field % 2 * LOW_ROWS : (field % 2 + 1) * LOW_ROWS,
                high * width : (high + 1) * width,
            ] = table_ref[
                high * LOW_ROWS : (high + 1) * LOW_ROWS, field * width : (field + 1) * width
            ]

    ahead = 7
    for field in range(min(ahead, fields)):
        pack(field)
    every(lambda step: ids_copy(step).wait_recv())
    for source in range(count):
        asked_rows_ref[:, source * slots : (source + 1) * slots] = ids_came_ref[source]
    asked_out_ref[...] = asked_rows_ref[...]
    asked_low = (asked_rows_ref[...] & 255).astype(WIDE).T.astype(LOW)
    asked_high = (asked_rows_ref[...] >> 8).astype(WIDE).T.astype(LOW)

    high_of = (lax.broadcasted_iota(jnp.int32, (1, wide), 1) // width).astype(WIDE).astype(LOW)
    column = lax.broadcasted_iota(jnp.int32, (wide, 1), 0)
    column = (column - column // width * width).astype(WIDE).astype(LOW)
    lane = lax.broadcasted_iota(jnp.int32, (1, 2 * LANES), 1)
    low_lane = counting((1, LOW_ROWS), 1)
    totals = [None] * (chunks + 1)
    done = 0
    for field in range(fields):
        if 4 <= field and field + ahead - 4 < fields:
            pack(field + ahead - 4)
        pick = equal(asked_low[:, field : field + 1], low_lane)
        half_at = field % 2 * LOW_ROWS
        blocks = product(pick, packed[field // 2, half_at : half_at + LOW_ROWS, :wide]).astype(LOW)
        blocks = jnp.where(
            asked_high[:, field : field + 1] == high_of, blocks, jnp.zeros((), LOW)
        )
        start = tile_of(field, width)
        fold = equal((lane - (field * width - start)).astype(WIDE).astype(LOW), column)
        rows = product(blocks, fold)
        for piece in range(2):
            part = rows[:, piece * LANES : (piece + 1) * LANES]
            at = start // LANES + piece
            totals[at] = part if totals[at] is None else totals[at] + part
        while done < ready_after(field, fields, width, chunks):
            whole = totals[done].astype(LOW)
            for target in range(count):
                found_ref[done, target] = whole[target * slots : (target + 1) * slots]
            chunk = done
            every(lambda step: rows_copy(chunk, step).start())
            came_ref[chunk, place] = found_ref[chunk, place]
            done += 1

    for part in range(points // LOW_ROWS):
        keys = jnp.concatenate([key_of(place_rows, part), spare.astype(WIDE)], axis=0)
        place_keys_ref[part] = keys.T.astype(LOW)
    marks = jnp.concatenate([here.astype(WIDE), spare.astype(WIDE)], axis=0).T.astype(LOW)
    on = presence_ref[fields_all:, :].astype(WIDE)
    spare = jnp.zeros((16 - dense, examples), WIDE)
    tail_all_ref[...] = (
        jnp.concatenate([dense_ref[...] * on, spare], axis=0).T[:, :dense].astype(LOW)
    )
    spare = jnp.zeros((7, examples), WIDE)
    label_col_ref[...] = jnp.concatenate([label_ref[...], spare], axis=0).T[:, 0:1]
    head_ref[mine] = jnp.concatenate([out_embed_ref[...], jnp.zeros((7, local), WIDE)], axis=0)
    send(2, head_ref.at[mine], head_ref.at[mine])

    raw_load.wait()
    for start in range(0, full, LANES):
        rows = min(LANES, full - start)
        both = layers_apart(raw_ref[start : start + rows])
        for layer in range(2):
            w_cross_ref[mine, layer, start : start + rows, :] = both[
                layer * rows : (layer + 1) * rows
            ]
    send(3, w_cross_ref.at[mine], w_cross_ref.at[mine])
    both = layers_apart(cross_tail_ref[...])
    for layer in range(2):
        w_tail_ref[layer] = both[layer * dense : (layer + 1) * dense]
    for ref in (x1_all_ref, x1_send_ref):
        ref[...] = jnp.zeros_like(ref)

    @pl.when(place == 0)
    def _():
        first_rows_ref[...] = table_ref[0:16, :]

    @pl.when(place != 0)
    def _():
        row_copy(1).wait_recv()

    kept = spread_of(marks[:, :fields], width, span) > 0.5
    for chunk in range(chunks):
        every(lambda step: rows_copy(chunk, step).wait_recv())
        got = came_ref[chunk].reshape(points, LANES)
        value = jnp.zeros((examples, LANES), WIDE)
        for field in range(fields):
            if field * width >= (chunk + 1) * LANES or (field + 1) * width <= chunk * LANES:
                continue
            order = jnp.concatenate(
                [
                    equal(place_keys_ref[part, :, field : field + 1], low_lane)
                    for part in range(points // LOW_ROWS)
                ],
                axis=1,
            )
            value = jnp.where(inside(field, width, chunk), product(order, got), value)
        end = min((chunk + 1) * LANES, local)
        default = first_rows_ref[0:1, chunk * LANES : end].astype(WIDE)
        if end < (chunk + 1) * LANES:
            default = jnp.concatenate(
                [default, jnp.zeros((1, (chunk + 1) * LANES - end), WIDE)], axis=1
            )
        tile = slice(chunk * LANES, (chunk + 1) * LANES)
        emb_all_ref[:, tile] = jnp.where(kept[:, tile], value, default).astype(LOW)
    send(4, emb_all_ref.at[peer_rows], x_parts_ref.at[mine])
    x_parts_ref[mine] = emb_all_ref[my_rows, :]
    low_tail = tail_all_ref[my_rows, :]
    deep_load.wait()
    second_load.wait()

    mixed = (
        product_t(x_parts_ref[mine, :, :local], w_cross_ref[mine, 0])
        + product(low_tail, w_tail_ref[0])
        + cross_bias_ref[0:1, :]
    )
    hidden_sum = (
        product(x_parts_ref[mine, :, :local], w_deep_ref[mine])
        + product(low_tail, deep_tail_ref[...])
        + deep_bias_ref[0:1, :]
    )
    for number in range(5):
        pair[number].wait_recv()
    mix_one_ref[...] = mixed + product_t(x_parts_ref[peer, :, :local], w_cross_ref[peer, 0])
    pre_one_ref[...] = hidden_sum + product(x_parts_ref[peer, :, :local], w_deep_ref[peer])
    out_cross = jnp.concatenate(
        [head_ref[0, 0:1, :], head_ref[1, 0:1, :], out_dense_ref[...]], axis=1
    )

    def rows_of(step):
        inner = pl.ds(pl.multiple_of(step * CHUNK, CHUNK), CHUNK)
        outer = pl.ds(pl.multiple_of(mine * half + step * CHUNK, CHUNK), CHUNK)
        return inner, outer

    def first_chunk(step, unused):
        inner, outer = rows_of(step)
        low = tail_all_ref[outer, :].astype(WIDE)
        x0 = jnp.concatenate(
            [
                x_parts_ref[0, inner, :local].astype(WIDE),
                x_parts_ref[1, inner, :local].astype(WIDE),
                low,
            ],
            axis=1,
        )
        anchor_ref[inner, :] = x0
        x1 = x0 * mix_one_ref[inner, :] + x0
        state_ref[inner, :] = x1
        one, two, end = x1[:, :local], x1[:, local:embed], x1[:, embed:]
        x1_parts_ref[0, inner, :] = one.astype(LOW)
        x1_parts_ref[1, inner, :] = two.astype(LOW)
        x1_tail_ref[inner, :] = end.astype(LOW)
        x1t_all_ref[outer, :] = end.astype(LOW)
        x1_all_ref[outer, :local] = jnp.where(first, one, two).astype(LOW)
        x1_send_ref[inner, :local] = jnp.where(first, two, one).astype(LOW)
        act, grad = gelu_parts(pre_one_ref[inner, :])
        slope_one_ref[inner, :] = grad
        h_low_ref[inner, :] = act.astype(LOW)
        one, two = act[:, :hidden], act[:, hidden:]
        h_all_ref[outer, :] = jnp.where(first, one, two).astype(LOW)
        h_send_ref[inner, :] = jnp.where(first, two, one).astype(LOW)
        return unused

    lax.fori_loop(0, half // CHUNK, first_chunk, 0)
    send(5, x1_send_ref, x1_all_ref.at[my_rows])
    send(6, h_send_ref, h_all_ref.at[my_rows])
    send(7, x1_tail_ref, x1t_all_ref.at[my_rows])

    mix_two_ref[...] = (
        product_t(x1_parts_ref[0], w_cross_ref[0, 1])
        + product_t(x1_parts_ref[1], w_cross_ref[1, 1])
        + product(x1_tail_ref[...], w_tail_ref[1])
        + cross_bias_ref[1:2, :]
    )
    pre_two_ref[...] = (
        product(h_low_ref[:, :hidden], w_second_ref[0])
        + product(h_low_ref[:, hidden:], w_second_ref[1])
        + deep_bias_ref[1:2, :]
    )

    def second_chunk(step, sums):
        sum_cross, sum_deep, sum_bias = sums
        inner, outer = rows_of(step)
        x0 = anchor_ref[inner, :]
        x2 = x0 * mix_two_ref[inner, :] + state_ref[inner, :]
        act, grad = gelu_parts(pre_two_ref[inner, :])
        logit = (
            jnp.sum(x2 * out_cross, axis=1, keepdims=True)
            + jnp.sum(act * out_deep_ref[...], axis=1, keepdims=True)
            + out_bias_ref[0]
        )
        g = 1.0 / (1.0 + jnp.exp(-logit)) - label_col_ref[outer, :]
        g_col_ref[inner, :] = g
        da_two_ref[outer, :] = ((g * out_deep_ref[...]) * grad).astype(LOW)
        dz_two_ref[outer, :] = ((g * out_cross) * x0).astype(LOW)
        return (
            sum_cross + jnp.sum(x2 * g, axis=0, keepdims=True),
            sum_deep + jnp.sum(act * g, axis=0, keepdims=True),
            sum_bias + jnp.sum(g, axis=0, keepdims=True),
        )

    sum_cross, sum_deep, sum_bias = lax.fori_loop(
        0,
        half // CHUNK,
        second_chunk,
        (jnp.zeros((1, full), WIDE), jnp.zeros((1, main), WIDE), jnp.zeros((1, 1), WIDE)),
    )
    send(8, dz_two_ref.at[my_rows], dz_two_ref.at[my_rows])
    send(9, da_two_ref.at[my_rows], da_two_ref.at[my_rows])
    part_send_ref[...] = jnp.zeros_like(part_send_ref)
    part_send_ref[0:1, :] = sum_cross
    part_send_ref[1:2, :main] = sum_deep
    part_send_ref[2:3, 0:1] = sum_bias
    send(10, part_send_ref, part_recv_ref)

    grad = da_two_ref[my_rows, :]
    back_hidden_ref[:, :hidden] = product_t(grad, w_second_ref[0])
    back_hidden_ref[:, hidden:] = product_t(grad, w_second_ref[1])
    grad = dz_two_ref[my_rows, :]
    back_one_ref[:, :local] = product(grad, w_cross_ref[0, 1])
    back_one_ref[:, local:embed] = product(grad, w_cross_ref[1, 1])
    back_one_ref[:, embed:] = product_t(grad, w_tail_ref[1])

    def third_chunk(step, unused):
        inner, outer = rows_of(step)
        dh = back_hidden_ref[inner, :].astype(LOW).astype(WIDE)
        da_one_ref[outer, :] = (dh * slope_one_ref[inner, :]).astype(LOW)
        dx2 = g_col_ref[inner, :] * out_cross
        dx1 = back_one_ref[inner, :] + dx2
        dz_one_ref[outer, :] = (dx1 * anchor_ref[inner, :]).astype(LOW)
        state_ref[inner, :] = dx1 + dx1 * mix_one_ref[inner, :] + dx2 * mix_two_ref[inner, :]
        return unused

    def bit_of(bit):
        return lax.rem(lax.div(place, 2**bit), 2)

    def partner(bit):
        return place + (1 - 2 * bit_of(bit)) * 2**bit

    units = units_ref.shape[0]

    def stream_of(at):
        order, delay = streams[at]
        acc, whole, got = (
            (rest_low_ref, rest_all_ref, rest_got_ref)
            if at == units
            else (units_ref.at[at], units_all_ref.at[at, :, pl.ds(0, span)], units_got_ref.at[at])
        )
        return {
            "at": at,
            "delay": delay,
            "acc": acc,
            "whole": whole,
            "came": got,
            "steps": plan_of(acc.shape[0], order),
            "turn": 0,
            "low": 0,
            "size": acc.shape[0],
            "filled": 0,
            "joined": False,
            "sent": [],
        }

    def link(one, source, target, other_place):
        turn = one["turn"]
        one["turn"] += 1
        copy = pltpu.make_async_remote_copy(
            src_ref=source,
            dst_ref=target,
            send_sem=sum_send_ref.at[one["at"], turn],
            recv_sem=sum_recv_ref.at[one["at"], turn],
            device_id={"dp": other_place},
            device_id_type=MESH,
        )
        copy.start()
        one["copies"].append(copy)

    def rows_at(low, size):
        return pl.ds(pl.multiple_of(low, 16), size)

    def quarter(bit, turn):
        own = lax.rem(lax.div(place, 2**bit), 4)
        high, low = lax.div(own, 2), lax.rem(own, 2)
        if turn & 1:
            low = 1 - low
        if turn & 2:
            high = 1 - high
        return own, 2 * high + low

    def start(one, step):
        kind, bit, size = one["steps"][step]
        one["copies"] = []
        low = one["low"]
        if kind in ("join", "gather"):
            settle(one)
            source = one["whole"].at[rows_at(low, size)]
            if kind == "join":
                link(one, source, source, partner(bit))
            else:
                for turn in (1, 2, 3):
                    own, reached = quarter(bit, turn)
                    link(one, source, source, place + (reached - own) * 2**bit)
            return
        one["got"] = one["filled"]
        if kind == "spread":
            for turn in (1, 2, 3):
                own, reached = quarter(bit, turn)
                source = one["acc"].at[rows_at(low + reached * size, size)]
                target = one["came"].at[pl.ds(one["filled"], size)]
                one["filled"] += size
                link(one, source, target, place + (reached - own) * 2**bit)
            one["low"] = low + quarter(bit, 0)[0] * size
            one["size"] = size
            return
        give = low
        if kind == "halve":
            side = bit_of(bit)
            give = low + (1 - side) * size
            one["low"] = low + side * size
            one["size"] = size
        target = one["came"].at[pl.ds(one["filled"], size)]
        one["filled"] += size
        link(one, one["acc"].at[rows_at(give, size)], target, partner(bit))

    def finish(one, step):
        kind, bit, size = one["steps"][step]
        for copy in one["copies"]:
            if kind == "both":
                copy.wait()
            else:
                copy.wait_recv()
                one["sent"].append(copy)
        if kind == "join":
            one["low"] = one["low"] - bit_of(bit) * size
        elif kind == "gather":
            one["low"] = one["low"] - quarter(bit, 0)[0] * size
        else:
            add(one, size, copies_in(one["steps"][step]))

    def add(one, size, parts):
        acc, low, got, came = one["acc"], one["low"], one["got"], one["came"]
        chunk = min(size, 64)

        def chunk_sum(step, unused):
            rows = rows_at(low + step * chunk, chunk)
            if parts == 1:
                acc[rows, :] = acc[rows, :] + came[rows_at(got + step * chunk, chunk), :]
            else:
                total = acc[rows, :].astype(WIDE)
                for part in range(parts):
                    taken = rows_at(got + part * size + step * chunk, chunk)
                    total = total + came[taken, :].astype(WIDE)
                acc[rows, :] = total.astype(LOW)
            return unused

        lax.fori_loop(0, size // chunk, chunk_sum, 0)

    def settle(one):
        if not one["joined"]:
            one["joined"] = True
            rows = rows_at(one["low"], one["size"])
            one["whole"][rows, :] = one["acc"][rows, :]

    small_copies, stores = [], []

    def small_step(step):
        if step > 0:
            small_copies[step - 1].wait_recv()
            small_acc_ref[step] = small_acc_ref[step - 1] + small_got_ref[step - 1]
        if step < bits:
            small_copies.append(
                pltpu.make_async_remote_copy(
                    src_ref=small_acc_ref.at[step],
                    dst_ref=small_got_ref.at[step],
                    send_sem=small_send_ref.at[step],
                    recv_sem=small_recv_ref.at[step],
                    device_id={"dp": partner(bits - 1 - step)},
                    device_id_type=MESH,
                )
            )
            small_copies[-1].start()

    def take(one, step):
        if step > 0:
            finish(one, step - 1)
        if step < len(one["steps"]):
            start(one, step)
            return
        settle(one)
        if one["at"] < units:
            stores.append(
                pltpu.make_async_copy(
                    one["whole"], units_out_ref.at[one["at"]], store_sem_ref.at[one["at"]]
                )
            )
            stores[-1].start()

    rest = rest_ref
    rest[...] = jnp.zeros_like(rest)

    def cross_units(layer, inputs, tails, grads):
        for block in range(main // UNIT):
            units_ref[layer * (main // UNIT) + block] = product_tn(
                grads[:, block * UNIT : (block + 1) * UNIT], inputs[...]
            ).astype(LOW)

    def cross_rest(layer, inputs, tails, grads):
        rest[layer * dense : (layer + 1) * dense, :] = product_tn(tails[...], grads[...])[
            :, :main
        ]
        ends = grads[:, main:]
        row = 3 * dense + layer * (full - main)
        rest[row : row + full - main, :span] = product_tn(ends, inputs[...])
        rest[row : row + full - main, span : span + dense] = product_tn(ends, tails[...])

    def deep_units(start, inputs, grads):
        for block in range(hidden // UNIT):
            found = product_tn(inputs[:, block * UNIT : (block + 1) * UNIT], grads[...])
            for side in range(2):
                units_ref[start + 2 * block + side] = found[
                    :, side * span : (side + 1) * span
                ].astype(LOW)

    def bias_of(grads):
        return jnp.sum(grads[...].astype(WIDE), axis=0, keepdims=True)

    def back_copy(step):
        return pltpu.make_async_remote_copy(
            src_ref=found_ref.at[:, other(step)],
            dst_ref=back_ref.at[:, place],
            send_sem=back_send_ref.at[step],
            recv_sem=back_recv_ref.at[step],
            device_id={"dp": other(step)},
            device_id_type=MESH,
        )
    low_row = counting((LOW_ROWS, 1), 0)

    def top_two():
        for number in (5, 7, 8):
            pair[number].wait_recv()
        cross_units(1, x1_all_ref, x1t_all_ref, dz_two_ref)

    def second_two():
        for number in (6, 9):
            pair[number].wait_recv()
        deep_units(6, h_all_ref, da_two_ref)

    def slopes():
        lax.fori_loop(0, half // CHUNK, third_chunk, 0)
        send(11, da_one_ref.at[my_rows], da_one_ref.at[my_rows])
        send(12, dz_one_ref.at[my_rows], dz_one_ref.at[my_rows])

    def layer_one():
        cross_grad = dz_one_ref[my_rows, :]
        deep_grad = da_one_ref[my_rows, :]
        back = back_one_ref
        for blk in range(2):
            back[:, blk * local : (blk + 1) * local] = product(
                cross_grad, w_cross_ref[blk, 0]
            ) + product_t(deep_grad, w_deep_ref[blk])
        back[:, embed:] = product_t(cross_grad, w_tail_ref[0]) + product_t(
            deep_grad, deep_tail_ref[...]
        )

        def fourth_chunk(step, unused):
            inner, outer = rows_of(step)
            value = back[inner, :] + state_ref[inner, :]
            one, two = value[:, :local], value[:, local:embed]
            ge_all_ref[outer, :local] = jnp.where(first, one, two).astype(LOW)
            h_send_ref[inner, :local] = jnp.where(first, two, one).astype(LOW)
            gd_all_ref[outer, :] = value[:, embed:]
            return unused

        pair[6].wait_send()
        lax.fori_loop(0, half // CHUNK, fourth_chunk, 0)
        send(13, h_send_ref, ge_all_ref.at[my_rows])
        send(14, gd_all_ref.at[my_rows], gd_all_ref.at[my_rows])

    def deep_one():
        pair[11].wait_recv()
        deep_units(4, emb_all_ref, da_one_ref)

    def top_one():
        pair[12].wait_recv()
        cross_units(0, emb_all_ref, tail_all_ref, dz_one_ref)

    def remainder():
        cross_rest(1, x1_all_ref, x1t_all_ref, dz_two_ref)
        cross_rest(0, emb_all_ref, tail_all_ref, dz_one_ref)
        rest[2 * dense : 3 * dense, :] = product_tn(tail_all_ref[...], da_one_ref[...])
        across = rest_low_ref.shape[1]
        for up in range(REST_ROWS // 16):
            for side in range(main // across):
                at = (up * (main // across) + side) * 16
                rest_low_ref[at : at + 16, :] = rest[
                    up * 16 : (up + 1) * 16, side * across : (side + 1) * across
                ].astype(LOW)
        filled = REST_ROWS * main // across
        rest_low_ref[filled:, :] = jnp.zeros((REST_UNIT - filled, across), LOW)

    def row_grads():
        small = small_acc_ref.at[0]
        small[...] = jnp.zeros((8, full), WIDE)
        small[0:1, :] = bias_of(dz_one_ref)
        small[1:2, :] = bias_of(dz_two_ref)
        small[2:3, :main] = bias_of(da_one_ref)
        small[3:4, :main] = bias_of(da_two_ref)
        pair[10].wait_recv()
        small[4:7, :] = part_send_ref[0:3, :] + part_recv_ref[0:3, :]
        pair[13].wait_recv()
        pair[14].wait_recv()
        grads = ge_all_ref[:, :local].astype(WIDE)
        kept = spread_of(marks[:, :fields], width, local) > 0.5
        small[7:8, :local] = jnp.sum(jnp.where(kept, 0.0, grads), axis=0, keepdims=True)
        grads = jnp.concatenate(
            [jnp.where(kept, grads, 0.0).astype(LOW), jnp.zeros((examples, span - local), LOW)], axis=1
        )

        def ordered(field, start, wide):
            order = jnp.concatenate(
                [
                    equal(key_of(place_rows[field : field + 1, :], part).astype(LOW), low_row)
                    for part in range(points // LOW_ROWS)
                ],
                axis=0,
            )
            return product(order, grads[:, start : start + wide])

        moved = by_field(fields, width, chunks, ordered).astype(LOW)
        for chunk in range(chunks):
            every(lambda step: rows_copy(chunk, step).wait_send())
        for chunk in range(chunks):
            for target in range(count):
                found_ref[chunk, target] = moved[
                    target * slots : (target + 1) * slots, chunk * LANES : (chunk + 1) * LANES
                ]
        embed_out_ref[...] = ge_all_ref[:, :local]
        spare = jnp.zeros((examples, 16 - dense), WIDE)
        dense_out_ref[...] = jnp.concatenate([gd_all_ref[...], spare], axis=1).T[:dense, :]
        every(lambda step: back_copy(step).start())
        for chunk in range(chunks):
            back_ref[chunk, place] = found_ref[chunk, place]

    stages = (pre_one_ref, pre_two_ref, slope_one_ref, back_hidden_ref)
    halves = [(ref, side) for ref in stages for side in range(main // span)]
    block_rows, blocks_here, unused = shares_of(table_rows)
    parts = block_rows // LOW_ROWS
    table_copies = []

    def table_block(block):
        value = scattered(asked_rows_ref, back_ref, block * parts, parts, fields, width)
        if block == 0:
            row = lax.broadcasted_iota(jnp.int32, (block_rows, 1), 0)
            extra = jnp.concatenate(
                [small_acc_ref[bits, 7:8, :local], jnp.zeros((1, span - local), WIDE)], axis=1
            )
            value = value + jnp.where((row == 0) & (place == 0), extra, 0.0)
        for part in range(parts):
            number, turn = block * parts + part, len(table_copies)
            if turn >= len(halves):
                table_copies[turn - len(halves)].wait()
            ref, side = halves[turn % len(halves)]
            stage = ref.at[:, pl.ds(side * span, span)]
            stage[...] = value[part * LOW_ROWS : (part + 1) * LOW_ROWS]
            table_copies.append(
                pltpu.make_async_copy(
                    stage,
                    table_out_ref.at[pl.ds(number * LOW_ROWS, LOW_ROWS)],
                    table_sem_ref.at[number],
                )
            )
            table_copies[-1].start()

    def next_block():
        if not table_copies:
            every(lambda step: back_copy(step).wait_recv())
            stores.append(pltpu.make_async_copy(back_ref, back_out_ref, back_store_ref))
            stores[-1].start()
        if blocks:
            table_block(blocks.pop())

    blocks = list(range(blocks_here))
    works = [top_two, second_two, slopes, layer_one, deep_one, top_one, remainder, row_grads]
    works += [next_block] * len(blocks)
    moment = list(moments[: len(works)])
    small_from = streams[units + 1][1]
    moment[-1] = max(moment[-1], small_from + bits + 1)
    running = [stream_of(at) for at in range(units + 1)]
    turns = [
        (one["delay"] + step, 1, one["delay"], one["at"], step)
        for one in running
        for step in range(len(one["steps"]) + 1)
    ]
    turns += [(small_from + step, 1, small_from, units + 1, step) for step in range(bits + 1)]
    turns += [(when, 0, number, 0, 0) for number, when in enumerate(moment)]
    for when, kind, number, at, step in sorted(turns):
        if kind == 0:
            works[number]()
        elif at > units:
            small_step(step)
        else:
            take(running[at], step)
    rest_out_ref[...] = rest_all_ref[...]
    small_out_ref[...] = small_acc_ref[bits]

    every(lambda step: ids_copy(step).wait_send())

    @pl.when(place == 0)
    def _():
        every(lambda step: row_copy(step).wait_send())

    for number in range(15):
        if number != 6:
            pair[number].wait_send()
    for copy in small_copies:
        copy.wait_send()
    for one in running:
        for copy in one["sent"]:
            copy.wait_send()
    every(lambda step: back_copy(step).wait_send())
    for copy in table_copies[-len(halves) :]:
        copy.wait()
    for store in stores:
        store.wait()


def train_part(arrays, count):
    ids, presence, dense, label, tables, cross, deep, second = arrays[:8]
    fields_all, examples = ids.shape
    fields = fields_all // 2
    table_rows, local = tables.shape
    width = local // fields
    half = examples // 2
    full = cross.shape[0]
    hidden, main = second.shape
    tails = dense.shape[0]
    slots = max(examples // count, 16)
    points = count * slots
    padded = -(-fields // 8) * 8
    chunks = -(-local // LANES)
    span = chunks * LANES
    bits = count.bit_length() - 1
    units = 4 * (main // UNIT)
    across = 256
    block_rows, blocks_here, unused = shares_of(table_rows)
    order = tuple(range(bits))
    swapped = (1, 0) + order[2:] if bits > 1 else order
    late = order[bits // 2 :] + order[: bits // 2]
    if bits == 4:
        straight, crossed = (0, 1, (2,)), (1, 0, (2,))
    else:
        straight, crossed = order, swapped
    kinds = (order, crossed, straight, swapped)
    delays = (3, 3, 0, 0, 5, 5, 1, 1)
    chosen = (3, 0, 2, 1, 1, 2, 3, 0)
    streams = [(kinds[kind], delay) for kind, delay in zip(chosen, delays)]
    streams += [(late, 3), (late, 5)]
    moments = (0, 1, 1, 1, 2, 2, 2, 4, 8, 11, 11)
    plans = [plan_of(UNIT, one) for one, delay in streams]
    held = max(held_rows(UNIT, one) for one, delay in streams)
    rest_held = held_rows(REST_UNIT, late)
    depth = max(sum(copies_in(step) for step in plan) for plan in plans)
    vmem = pl.BlockSpec(memory_space=pltpu.VMEM)
    anywhere = pl.BlockSpec(memory_space=pl.ANY)
    wide_rows = -(-(table_rows // LOW_ROWS * width) // LANES) * LANES
    dma = pltpu.SemaphoreType.DMA

    def kernel(*refs):
        train_kernel(streams, moments, *refs)

    return pl.pallas_call(
        kernel,
        out_shape=(
            jax.ShapeDtypeStruct((units, UNIT, span), LOW),
            jax.ShapeDtypeStruct((REST_UNIT, across), LOW),
            jax.ShapeDtypeStruct((8, full), WIDE),
            jax.ShapeDtypeStruct((examples, local), LOW),
            jax.ShapeDtypeStruct((tails, examples), WIDE),
            jax.ShapeDtypeStruct((block_rows * blocks_here, span), WIDE),
            jax.ShapeDtypeStruct((padded, points), jnp.int32),
            jax.ShapeDtypeStruct((chunks, count, slots, LANES), LOW),
        ),
        in_specs=[vmem] * 4
        + [anywhere] * 4
        + [vmem] * 7
        + [pl.BlockSpec(memory_space=pltpu.SMEM)],
        out_specs=[anywhere] + [vmem] * 4 + [anywhere, vmem, anywhere],
        scratch_shapes=[
            pltpu.VMEM((table_rows, local), LOW),
            pltpu.VMEM((chunks, count, slots, LANES), LOW),
            pltpu.VMEM((chunks, count, slots, LANES), LOW),
            pltpu.VMEM((16, local), LOW),
            pltpu.VMEM((count, padded, slots), jnp.int32),
            pltpu.VMEM((padded, points), jnp.int32),
            pltpu.VMEM((count, padded, slots), jnp.int32),
            pltpu.VMEM((full, 2, local), LOW),
            pltpu.VMEM((2, 2, full, local), LOW),
            pltpu.VMEM((2, local, main), LOW),
            pltpu.VMEM((2, hidden, main), LOW),
            pltpu.VMEM((2, tails, full), LOW),
            pltpu.VMEM((2, 8, local), WIDE),
            pltpu.VMEM((examples, span), LOW),
            pltpu.VMEM((examples, tails), LOW),
            pltpu.VMEM((2, half, span), LOW),
            pltpu.VMEM((2, half, local), LOW),
            pltpu.VMEM((half, tails), LOW),
            pltpu.VMEM((half, main), LOW),
            pltpu.VMEM((half, full), WIDE),
            pltpu.VMEM((half, full), WIDE),
            pltpu.VMEM((half, full), WIDE),
            pltpu.VMEM((half, full), WIDE),
            pltpu.VMEM((half, main), WIDE),
            pltpu.VMEM((half, main), WIDE),
            pltpu.VMEM((half, main), WIDE),
            pltpu.VMEM((half, full), WIDE),
            pltpu.VMEM((half, main), WIDE),
            pltpu.VMEM((half, 1), WIDE),
            pltpu.VMEM((examples, 1), WIDE),
            pltpu.VMEM((examples, span), LOW),
            pltpu.VMEM((examples, tails), LOW),
            pltpu.VMEM((half, span), LOW),
            pltpu.VMEM((examples, hidden), LOW),
            pltpu.VMEM((half, hidden), LOW),
            pltpu.VMEM((examples, full), LOW),
            pltpu.VMEM((examples, full), LOW),
            pltpu.VMEM((examples, main), LOW),
            pltpu.VMEM((examples, main), LOW),
            pltpu.VMEM((examples, span), LOW),
            pltpu.VMEM((examples, tails), WIDE),
            pltpu.VMEM((8, full), WIDE),
            pltpu.VMEM((8, full), WIDE),
            pltpu.VMEM((REST_ROWS, main), WIDE),
            pltpu.VMEM((chunks, count, slots, LANES), LOW),
            pltpu.VMEM((points // LOW_ROWS, examples, padded), LOW),
            pltpu.VMEM((units, UNIT, span), LOW),
            pltpu.VMEM((REST_UNIT, across), LOW),
            pltpu.VMEM((max(units, -(-fields // 2)), UNIT, max(wide_rows, span)), LOW),
            pltpu.VMEM((REST_UNIT, across), LOW),
            pltpu.VMEM((units, held, span), LOW),
            pltpu.VMEM((rest_held, across), LOW),
            pltpu.VMEM((bits + 1, 8, full), WIDE),
            pltpu.VMEM((bits, 8, full), WIDE),
            dma((4,)),
            dma((count,)),
            dma((count,)),
            dma((chunks, count)),
            dma((chunks, count)),
            dma((count,)),
            dma,
            dma((15,)),
            dma((15,)),
            dma((units + 1, depth)),
            dma((units + 1, depth)),
            dma((bits,)),
            dma((bits,)),
            dma((units,)),
            dma((count,)),
            dma((count,)),
            dma((table_rows // LOW_ROWS,)),
            dma,
        ],
        compiler_params=pltpu.CompilerParams(
            collective_id=1, has_side_effects=True, vmem_limit_bytes=63 * 2**20
        ),
        cost_estimate=pl.CostEstimate(
            flops=2 * 10**10, bytes_accessed=3 * 10**7, transcendentals=10**6
        ),
    )(*arrays)


def finish_kernel(
    fields,
    table,
    asked,
    back,
    units,
    rest,
    small,
    embed,
    dense,
    table_out,
    top_out,
    tail_out,
    deep_out,
    deep_tail_out,
    second_out,
    embed_out,
    dense_out,
    cross_bias_out,
    deep_bias_out,
    out_embed_out,
    out_dense_out,
    out_deep_out,
    out_bias_out,
    table_in,
    table_wide,
    units_in,
    embed_in,
    embed_wide,
    top_wide,
    deep_wide,
    second_wide,
    stage_end,
    stage_tail,
    ends,
    unit_sem,
    table_sem,
    embed_sem,
    out_sem,
    row_sem,
    block_sem,
):
    table_rows, local = table_wide.shape
    tails, main = deep_tail_out.shape
    full = top_out.shape[0]
    span = units.shape[2]
    blocks = main // UNIT
    total = units.shape[0]
    block_rows, blocks_before, blocks_here = shares_of(table_rows)
    copied = block_rows * blocks_before
    share = copied // total
    parts = block_rows // LOW_ROWS
    width = local // fields
    order = [layer * blocks + block for block in range(blocks) for layer in range(2)]
    order += list(range(2 * blocks, total))

    def unit_load(at):
        return pltpu.make_async_copy(units.at[at], units_in.at[at], unit_sem.at[at])

    def table_load(at):
        rows = pl.ds(at * share, share)
        return pltpu.make_async_copy(table.at[rows], table_in.at[rows], table_sem.at[at])

    outs = []

    def put(source, target):
        outs.append(pltpu.make_async_copy(source, target, out_sem.at[len(outs)]))
        outs[-1].start()

    embed_load = pltpu.make_async_copy(embed, embed_in, embed_sem)
    for number, at in enumerate(order):
        unit_load(at).start()
        table_load(number).start()
    embed_load.start()

    across = rest.shape[1]
    for up in range(REST_ROWS // 16):
        for side in range(main // across):
            at = (up * (main // across) + side) * 16
            ends[up * 16 : (up + 1) * 16, side * across : (side + 1) * across] = rest[
                at : at + 16, :
            ].astype(WIDE)
    for layer in range(2):
        start = 3 * tails + layer * (full - main)
        stage_end[layer] = ends[start : start + full - main, :local]
        stage_tail[layer, :, :main] = ends[layer * tails : (layer + 1) * tails, :]
        corner = ends[start : start + full - main, span : span + LANES]
        corner = jnp.concatenate([corner, jnp.zeros((8 - full + main, LANES), WIDE)], axis=0)
        stage_tail[layer, :, main:] = corner.T[:tails, : full - main]
        put(stage_end.at[layer], top_out.at[pl.ds(main, full - main), layer])
        put(stage_tail.at[layer], tail_out.at[:, layer])
    deep_tail_out[...] = ends[2 * tails : 3 * tails, :]
    dense_out[...] = dense[...]
    cross_bias_out[...] = small[0:2, :]
    deep_bias_out[...] = small[2:4, :main]
    out_embed_out[...] = jnp.where(
        lax.axis_index("mp") == 0, small[4:5, :local], small[4:5, local : 2 * local]
    )
    out_dense_out[...] = small[4:5, 2 * local :]
    out_deep_out[...] = small[5:6, :main]
    out_bias_out[...] = small[6:7, 0:1]

    def row_copy(at):
        rows = pl.ds(at * share, share)
        return pltpu.make_async_copy(table_wide.at[rows], table_out.at[rows], row_sem.at[at])

    def block_copy(block):
        rows = pl.ds(copied + block * block_rows, block_rows)
        return pltpu.make_async_copy(table_wide.at[rows], table_out.at[rows], block_sem.at[block])

    def table_block(block):
        start = copied + block * block_rows
        value = scattered(asked, back, start // LOW_ROWS, parts, fields, width)
        table_wide[start : start + block_rows, :] = value[:, :local]
        block_copy(block).start()

    for block in range(blocks_here):
        table_block(block)
    for number, at in enumerate(order):
        unit_load(at).wait()
        matrix, block = at // blocks, at % blocks
        if matrix < 2:
            top_wide[matrix, block] = units_in[at, :, :local].astype(WIDE)
            put(top_wide.at[matrix, block], top_out.at[pl.ds(block * UNIT, UNIT), matrix])
        else:
            target, result = ((deep_wide, deep_out), (second_wide, second_out))[matrix - 2]
            target[:, block * span : (block + 1) * span] = units_in[
                at, : target.shape[0], :
            ].astype(WIDE)
            if block == blocks - 1:
                put(target, result)
        table_load(number).wait()
        rows = slice(number * share, (number + 1) * share)
        table_wide[rows, :] = table_in[rows, :local]
        row_copy(number).start()
    embed_load.wait()
    embed_wide[...] = embed_in[...].astype(WIDE)
    put(embed_wide, embed_out)
    for copy in outs:
        copy.wait()
    for number in range(total):
        row_copy(number).wait()
    for block in range(blocks_here):
        block_copy(block).wait()


def finish_part(table, asked, back, units, rest, small, embed, dense, table_rows, fields, full):
    before, span = table.shape
    examples, local = embed.shape
    tails = dense.shape[0]
    total = units.shape[0]
    main = total // 4 * UNIT
    hidden = main // 2
    vmem = pl.BlockSpec(memory_space=pltpu.VMEM)
    anywhere = pl.BlockSpec(memory_space=pl.ANY)
    shapes = (
        (table_rows, local),
        (full, 2, local),
        (tails, 2, full),
        (local, main),
        (tails, main),
        (hidden, main),
        (examples, local),
        (tails, examples),
        (2, full),
        (2, main),
        (1, local),
        (1, tails),
        (1, main),
        (1, 1),
    )
    dma = pltpu.SemaphoreType.DMA

    def kernel(*refs):
        finish_kernel(fields, *refs)

    return pl.pallas_call(
        kernel,
        out_shape=tuple(jax.ShapeDtypeStruct(shape, WIDE) for shape in shapes),
        in_specs=[anywhere, vmem, vmem, anywhere, vmem, vmem, anywhere, vmem],
        out_specs=[anywhere] * 4 + [vmem] + [anywhere] * 2 + [vmem] * 7,
        scratch_shapes=[
            pltpu.VMEM((before, span), WIDE),
            pltpu.VMEM((table_rows, local), WIDE),
            pltpu.VMEM(units.shape, LOW),
            pltpu.VMEM((examples, local), LOW),
            pltpu.VMEM((examples, local), WIDE),
            pltpu.VMEM((2, total // 4, UNIT, local), WIDE),
            pltpu.VMEM((local, main), WIDE),
            pltpu.VMEM((hidden, main), WIDE),
            pltpu.VMEM((2, full - main, local), WIDE),
            pltpu.VMEM((2, tails, full), WIDE),
            pltpu.VMEM((REST_ROWS, main), WIDE),
            dma((total,)),
            dma((total,)),
            dma,
            dma((16,)),
            dma((total,)),
            dma((max(1, shares_of(table_rows)[2]),)),
        ],
        compiler_params=pltpu.CompilerParams(vmem_limit_bytes=60 * 2**20),
        cost_estimate=pl.CostEstimate(flops=10**7, bytes_accessed=31 * 10**6, transcendentals=0),
    )(table, asked, back, units, rest, small, embed, dense)


def local(
    field_ids,
    presence,
    dense,
    labels,
    tables,
    cross_top,
    cross_tail,
    cross_bias,
    deep_top,
    deep_tail,
    deep_second,
    deep_bias,
    out_embed,
    out_dense,
    out_deep,
    out_bias,
):
    count = lax.axis_size("dp")
    arrays = (
        field_ids.T,
        presence.T,
        dense.T,
        labels[None, :],
        tables,
        cross_top.transpose(2, 0, 1),
        deep_top,
        deep_second,
        cross_tail.transpose(1, 0, 2),
        cross_bias,
        deep_tail,
        deep_bias,
        out_embed[None, :],
        out_dense[None, :],
        out_deep[None, :],
        out_bias,
    )
    units, rest, small, embed, grad_dense, table_grads, asked, back = train_part(arrays, count)
    (
        grad_tables,
        top,
        tail,
        dtop,
        dtail,
        second,
        grad_embedded,
        grad_dense,
        cross_bias,
        deep_bias,
        oembed,
        odense,
        odeep,
        obias,
    ) = finish_part(
        table_grads,
        asked,
        back,
        units,
        rest,
        small,
        embed,
        grad_dense,
        tables.shape[0],
        field_ids.shape[1] // 2,
        cross_bias.shape[1],
    )
    return (
        grad_embedded,
        grad_dense.T,
        grad_tables,
        top.transpose(1, 2, 0),
        tail.transpose(1, 0, 2),
        cross_bias,
        dtop,
        dtail,
        second,
        deep_bias,
        oembed[0],
        odense[0],
        odeep[0],
        obias[0],
    )


def solution(mesh):
    in_specs = (
        P("dp", None),
        P("dp", None),
        P("dp", None),
        P("dp"),
        P("dp", "mp"),
        P(None, "mp", None),
        P(),
        P(),
        P("mp", None),
        P(),
        P("mp", None),
        P(),
        P("mp"),
        P(),
        P(),
        P(),
    )
    out_specs = (
        P("dp", "mp"),
        P("dp", None),
        P("dp", "mp"),
        P(None, "mp", None),
        P(),
        P(),
        P("mp", None),
        P(),
        P("mp", None),
        P(),
        P("mp"),
        P(),
        P(),
        P(),
    )
    return jax.shard_map(local, mesh=mesh, in_specs=in_specs, out_specs=out_specs, check_vma=False)
```
